512 devices in a mesh: blk: 32 (over x, y), pair: 16 (over z, core).
Axes of the slice: x: 4, y: 8, z: 8, core: 2. Of those that a mesh axis runs over, the one named last changes fastest.
Arguments:
- density: bfloat16 [96, 3, 128, 128], P('blk', None, 'pair'), may hold values from -6 to 6
- exponents: float32 [12288], replicated, may hold values from 0.1 to 1
- offsets: float32 [12288], replicated, may hold values from -3 to 3
- expansion: float32 [4, 12288], replicated, may hold values from -6 to 6
- quartet_list: int32 [32, 16, 4, 128], P('blk', 'pair'), may hold values from 0 to 95, as said below
- list_length: int32 [32, 16], P('blk', 'pair'), may hold values from 16 to 128, as said below
Outputs:
- exchange: float32 [96, 3, 128, 128], P('blk', None, 'pair')
The draws below stay inside these ranges and needn't reach their ends.
Inputs may be any that keep to these rules, and one draw needn't show every extreme that they name: `quartet_list`: every slot holds a quartet: the I of device (b, q) lies in blocks b * 3 to (b + 1) * 3 - 1, and |I - J|, |I - K|, |J - L|, |K - L| are each at most 1. Device (b, q) has the live quartets in its first list_length[b, q] slots; in every draw some device's list is full.
All inputs are finite; a program needn't handle non-finite values.
Results may differ from the reference program's by a relative error of at most 0.0047.
Values may be sent and summed in bfloat16 or wider, within the bound.
No kernel may reach another device: no remote copies, remote signals or barrier semaphores. Data moves between devices by JAX's collectives and lax.ppermute only.
A program may use at most 64 MiB of HBM per device.

```python
import math
import jax
import jax.numpy as jnp
from jax import lax

BS = 128
W = 1
NAUX = 4
BLK_DEV = 3
QCAP = 128
BAND = 3
NBLK = 96
NBASIS = 12288
N_BLK = 32
N_PAIR = 16


def draw_quartet_list(key, part):
    key = jax.random.fold_in(key, 11)
    keys = jax.random.split(key, 4)
    shape = (N_BLK, N_PAIR, QCAP)
    owner = jnp.arange(N_BLK, dtype=jnp.int32)[:, None, None]
    row_block = owner * BLK_DEV + jax.random.randint(keys[0], shape, 0, BLK_DEV)
    col_block = jnp.clip(row_block + jax.random.randint(keys[1], shape, -W, W + 1), 0, NBLK - 1)
    mid_block = jnp.clip(row_block + jax.random.randint(keys[2], shape, -W, W + 1), 0, NBLK - 1)
    lower = jnp.maximum(jnp.maximum(col_block - W, mid_block - W), 0)
    upper = jnp.minimum(jnp.minimum(col_block + W, mid_block + W), NBLK - 1)
    far_block = jnp.clip(mid_block + jax.random.randint(keys[3], shape, -W, W + 1), lower, upper)
    return jnp.stack([row_block, col_block, mid_block, far_block], axis=2).astype(jnp.int32)


def draw_list_length(key, part):
    key = jax.random.fold_in(key, 23)
    keys = jax.random.split(key, 2)
    level = jax.random.randint(keys[0], (N_BLK * N_PAIR,), 0, 8)
    base = QCAP // 8 + (QCAP - QCAP // 8) * level * level * level // 343
    chosen = jax.random.randint(keys[1], (), 0, N_BLK * N_PAIR)
    filled = jnp.where(jnp.arange(N_BLK * N_PAIR) == chosen, QCAP, base)
    return filled.reshape(N_BLK, N_PAIR).astype(jnp.int32)


def block_levels(own_key, dims, cuts, smallest, top_value):
    loudness = 1.0
    for axis_at, shards_of in cuts:
        steps = jax.random.uniform(jax.random.fold_in(jax.random.fold_in(own_key, 6), axis_at), (shards_of,), jnp.float32, smallest / len(cuts), top_value / len(cuts))
        loudness = loudness * jnp.repeat(jnp.exp(steps), dims[axis_at] // shards_of).reshape((-1,) + (1,) * (len(dims) - 1 - axis_at))
    return loudness


def normal_values(rng, dims, width, bound, cuts=(), held_as=jnp.bfloat16):
    result = jax.random.normal(rng, dims, jnp.float32) * width
    if len(cuts) > 0:
        result = block_levels(rng, dims, cuts, -0.22, 0.18) * result
    return jnp.clip(result, min=-bound, max=bound).astype(held_as)


def setup_inputs(seed: int = 0) -> dict:
    key_list = jax.random.split(jax.random.key(seed), 7)
    return {
        "density": normal_values(key_list[0], (NBLK, BAND, BS, BS), 1.0, 6.0, ((0, 32), (2, 16))),
        "exponents": jnp.clip(jnp.exp(jax.random.uniform(key_list[1], (NBASIS,), jnp.float32, math.log(0.1), math.log(1.0))), 0.1, 1.0),
        "offsets": jnp.clip(jax.random.uniform(key_list[2], (NBASIS,), jnp.float32, -3.0, 3.0), -3.0, 3.0),
        "expansion": normal_values(key_list[3], (NAUX, NBASIS), 1.5, 6.0, (), jnp.float32),
        "quartet_list": draw_quartet_list(jax.random.fold_in(key_list[6], 71), 0),
        "list_length": draw_list_length(jax.random.fold_in(key_list[6], 71), 0),
    }


def block_factors(rows_blk, cols_blk, expo_table, offset_table, weight_table):
    row_expo = jnp.take(expo_table, rows_blk, axis=0)
    column_expo = jnp.take(expo_table, cols_blk, axis=0)
    row_position = 2.0 * rows_blk.astype(jnp.float32)[:, None] + jnp.take(offset_table, rows_blk, axis=0)
    column_position = 2.0 * cols_blk.astype(jnp.float32)[:, None] + jnp.take(offset_table, cols_blk, axis=0)
    reduced = row_expo[:, :, None] * column_expo[:, None, :] / (row_expo[:, :, None] + column_expo[:, None, :])
    distance = row_position[:, :, None] - column_position[:, None, :]
    intersection = jnp.exp(-reduced * distance * distance)
    row_weight = jnp.moveaxis(jnp.take(weight_table, rows_blk, axis=1), 0, 1)
    column_weight = jnp.moveaxis(jnp.take(weight_table, cols_blk, axis=1), 0, 1)
    mixed = intersection[:, None] * jnp.tanh(row_weight[:, :, :, None] * column_weight[:, :, None, :])
    return mixed.astype(jnp.bfloat16)


def reference(density, exponents, offsets, expansion, quartet_list, list_length):
    expo_table = exponents.reshape(NBLK, BS)
    offset_table = offsets.reshape(NBLK, BS)
    weight_table = expansion.reshape(NAUX, NBLK, BS)
    flat_list = jnp.transpose(quartet_list, (0, 1, 3, 2)).reshape(-1, 4).astype(jnp.int32)
    slot_index = jnp.arange(QCAP, dtype=jnp.int32)
    alive_flags = (slot_index[None, None, :] < list_length[:, :, None]).reshape(-1)

    def visit_slot(running, slot_data):
        quartet, alive = slot_data

        def add_quartet(current):
            left_factor = block_factors(quartet[0:1], quartet[2:3], expo_table, offset_table, weight_table)[0]
            right_factor = block_factors(quartet[1:2], quartet[3:4], expo_table, offset_table, weight_table)[0]
            density_tile = density[quartet[2], quartet[3] - quartet[2] + W]
            half_product = jnp.einsum('pik,kl->pil', left_factor.astype(jnp.float32), density_tile.astype(jnp.float32)).astype(jnp.bfloat16)
            quartet_term = jnp.einsum('pil,pjl->ij', half_product.astype(jnp.float32), right_factor.astype(jnp.float32))
            column = quartet[1] - quartet[0] + W
            return current.at[quartet[0], column].add(quartet_term)

        def skip_quartet(current):
            return current

        return lax.cond(alive, add_quartet, skip_quartet, running), None

    start = jnp.zeros((NBLK, BAND, BS, BS), jnp.float32)
    running, unused = lax.scan(visit_slot, start, (flat_list, alive_flags))
    return running * 0.0078125
```

```python
import jax
import jax.numpy as jnp
from jax import lax
from jax.experimental import pallas as pl
from jax.experimental.pallas import tpu as pltpu
from jax.sharding import PartitionSpec as P

BS = 128
NAUX = 4
OWN = 3
BAND = 3
NEAR = OWN + 2
FAR = OWN + 4
ROWS = 8
SCALE = 0.0078125

LEFT_PAIRS = [(k, i) for k in range(NEAR) for i in range(OWN) if abs(i - (k - 1)) <= 1]
FIRST_LEFT = {pair: at for at, pair in enumerate(LEFT_PAIRS)}


def owners_of(near):
    return [i for i in range(OWN) if abs(i - (near - 1)) <= 1]


def factors_kernel(table_ref, list_ref, density_ref, right_ref, left_ref, own_ref, rows_ref, cols_ref):
    own_first = lax.axis_index("blk") * OWN
    my_row = pl.multiple_of(lax.axis_index("pair") * ROWS, ROWS)
    nblk = table_ref.shape[1] // BS

    rows_ref[...] = jnp.zeros_like(rows_ref)
    for t in range(FAR):
        block = jnp.clip(own_first - 2 + t, 0, nblk - 1)
        values = table_ref[:, pl.ds(pl.multiple_of(block * BS, BS), BS)]
        rows_ref[t : t + 1, :] = values[0:1, :]
        rows_ref[8 + t : 9 + t, :] = 2.0 * block.astype(jnp.float32) + values[1:2, :]
        for p in range(NAUX):
            rows_ref[16 + 8 * p + t : 17 + 8 * p + t, :] = values[2 + p : 3 + p, :]
    cols_ref[...] = rows_ref[...].T

    def tiles(columns, t_row, t_col):
        def column(quantity):
            at = 8 * quantity + t_row
            return columns[:, at : at + 1]

        def row(quantity):
            at = 8 * quantity + t_col
            return rows_ref[at : at + 1, :]

        e_r, e_c = column(0), row(0)
        reduced = e_r * e_c / (e_r + e_c)
        distance = column(1) - row(1)
        overlap = jnp.exp(-reduced * distance * distance)
        return [
            (overlap * jnp.tanh(column(2 + p) * row(2 + p))).astype(jnp.bfloat16)
            for p in range(NAUX)
        ]

    step = 32
    for t_far in range(FAR):
        for start in range(0, BS, step):
            columns = cols_ref[start : start + step, :]
            for near in range(NEAR):
                side = t_far - near
                if 0 <= side <= 2:
                    for p, tile in enumerate(tiles(columns, t_far, near + 1)):
                        at = (side * NAUX + p) * BS + start
                        right_ref[near, at : at + step, :] = tile

    mine = cols_ref[pl.ds(my_row, ROWS), :]
    for at, (near, own) in enumerate(LEFT_PAIRS):
        made = tiles(mine, own + 2, near + 1)
        left_ref[at * 32 : at * 32 + 32, :] = jnp.concatenate(made, axis=0)

    row_b, col_b, mid_b, far_b, length = (list_ref[n : n + 1, :] for n in range(5))
    code = (
        (row_b - own_first) * 27 + (col_b - row_b + 1) * 9 + (mid_b - row_b + 1) * 3 + far_b - mid_b + 1
    )
    slot = lax.broadcasted_iota(jnp.int32, (1, BS), 1)
    code = jnp.where(slot < length, code, BS)
    same = code == lax.broadcasted_iota(jnp.int32, (BS, BS), 0)
    first = lax.broadcasted_iota(jnp.int32, (ROWS, BS), 0) == 0
    counts = lax.dot_general(
        first.astype(jnp.float32).astype(jnp.bfloat16),
        same.astype(jnp.float32).astype(jnp.bfloat16),
        (((1,), (1,)), ((), ())),
        preferred_element_type=jnp.float32,
    )
    own_ref[OWN * BAND] = counts.astype(jnp.bfloat16)
    for tile in range(OWN * BAND):
        own_ref[tile] = density_ref[tile // BAND, tile % BAND]


def products_kernel(bank_ref, right_ref, left_ref, out_ref, half_ref, times_ref, mixed_ref):
    def bank(tile):
        return bank_ref[:, tile].astype(jnp.float32).reshape(BS, BS)

    totals = jnp.sum(bank(NEAR * BAND), axis=0, keepdims=True)
    times_ref[...] = jnp.broadcast_to(totals, (BS, BS)).T

    for near in range(NEAR):
        density = jnp.concatenate([bank(near * BAND + c) for c in range(BAND)], axis=1)
        density = density.astype(jnp.bfloat16)
        owners = owners_of(near)
        at = FIRST_LEFT[(near, owners[0])] * 32
        size = len(owners) * 32
        half = jnp.dot(left_ref[at : at + size, :], density, preferred_element_type=jnp.float32)
        half_ref[at : at + size, :] = half.astype(jnp.bfloat16).astype(jnp.float32)

    for j in range(NEAR):
        owners = owners_of(j)
        for slot, i in enumerate(owners):
            for side in range(3):
                far = j - 1 + side
                total = [None] * NAUX
                for k in range(i, i + 3):
                    if abs(far - k) > 1:
                        continue
                    code = i * 27 + (j - i) * 9 + (k - i) * 3 + far - k + 1
                    times = times_ref[code : code + 1, :]
                    at = FIRST_LEFT[(k, i)] * 32
                    column = (far - k + 1) * BS
                    for p in range(NAUX):
                        piece = times * half_ref[
                            at + p * ROWS : at + (p + 1) * ROWS, column : column + BS
                        ]
                        total[p] = piece if total[p] is None else total[p] + piece
                for p in range(NAUX):
                    high = total[p].astype(jnp.bfloat16)
                    low = total[p] - high.astype(jnp.float32)
                    both = jnp.concatenate([high.astype(jnp.float32), low], axis=0)
                    column = (side * NAUX + p) * BS
                    mixed_ref[slot * 16 : slot * 16 + 16, column : column + BS] = both.astype(
                        jnp.bfloat16
                    )
        size = len(owners) * 16
        term = jnp.dot(mixed_ref[:size, :], right_ref[j], preferred_element_type=jnp.float32)
        for slot, i in enumerate(owners):
            pair = term[slot * 16 : slot * 16 + 8] + term[slot * 16 + 8 : slot * 16 + 16]
            out_ref[i, j - i] = pair * SCALE


def vmem(count):
    return [pl.BlockSpec(memory_space=pltpu.VMEM)] * count


def shards(density, exponents, offsets, expansion, quartet_list, list_length):
    count = lax.axis_size("blk")
    forward = [(i, i + 1) for i in range(count - 1)]
    backward = [(i + 1, i) for i in range(count - 1)]
    low = lax.ppermute(density, "blk", forward)[OWN - 1]
    high = lax.ppermute(density, "blk", backward)[0]

    tables = jnp.concatenate([exponents[None], offsets[None], expansion], axis=0)
    listed = jnp.concatenate([quartet_list[0, 0], jnp.broadcast_to(list_length, (1, BS))], axis=0)
    right, left, own = pl.pallas_call(
        factors_kernel,
        out_shape=(
            jax.ShapeDtypeStruct((NEAR, 3 * NAUX * BS, BS), jnp.bfloat16),
            jax.ShapeDtypeStruct((len(LEFT_PAIRS) * NAUX * ROWS, BS), jnp.bfloat16),
            jax.ShapeDtypeStruct((OWN * BAND + 1, ROWS, BS), jnp.bfloat16),
        ),
        in_specs=vmem(3),
        out_specs=tuple(vmem(3)),
        scratch_shapes=[pltpu.VMEM((BS, BS), jnp.float32), pltpu.VMEM((BS, BS), jnp.float32)],
        compiler_params=pltpu.CompilerParams(vmem_limit_bytes=24 * 2**20),
        cost_estimate=pl.CostEstimate(flops=30_000_000, bytes_accessed=3_000_000, transcendentals=1_500_000),
        name="factors",
    )(tables, listed, density)

    payload = jnp.concatenate([low, own[: OWN * BAND], high, own[OWN * BAND :]], axis=0)
    pairs = lax.axis_size("pair")
    copies = jnp.broadcast_to(payload[None], (pairs,) + payload.shape)
    bank = lax.all_to_all(copies, "pair", split_axis=0, concat_axis=0, tiled=True)

    return pl.pallas_call(
        products_kernel,
        out_shape=jax.ShapeDtypeStruct((OWN, BAND, ROWS, BS), jnp.float32),
        in_specs=vmem(3),
        out_specs=pl.BlockSpec(memory_space=pltpu.VMEM),
        scratch_shapes=[
            pltpu.VMEM((len(LEFT_PAIRS) * NAUX * ROWS, BAND * BS), jnp.float32),
            pltpu.VMEM((BS, BS), jnp.float32),
            pltpu.VMEM((3 * 16, 3 * NAUX * BS), jnp.bfloat16),
        ],
        compiler_params=pltpu.CompilerParams(vmem_limit_bytes=24 * 2**20),
        name="products",
    )(bank, right, left)


def solution(mesh):
    return jax.shard_map(
        shards,
        mesh=mesh,
        in_specs=(
            P("blk", None, "pair", None),
            P(),
            P(),
            P(),
            P("blk", "pair", None, None),
            P("blk", "pair"),
        ),
        out_specs=P("blk", None, "pair", None),
        check_vma=False,
    )
```

```python
import jax
import jax.numpy as jnp
from jax import lax
from jax.experimental import pallas as pl
from jax.experimental.pallas import tpu as pltpu
from jax.sharding import PartitionSpec as P

BS = 128
NAUX = 4
OWN = 3
BAND = 3
NEAR = OWN + 2
FAR = OWN + 4
ROWS = 8
SCALE = 0.0078125

LEFT_PAIRS = [(k, i) for k in range(NEAR) for i in range(OWN) if abs(i - (k - 1)) <= 1]
FIRST_LEFT = {pair: at for at, pair in enumerate(LEFT_PAIRS)}


def owners_of(near):
    return [i for i in range(OWN) if abs(i - (near - 1)) <= 1]


def factors_kernel(table_ref, right_ref, left_ref, rows_ref, cols_ref):
    own_first = lax.axis_index("blk") * OWN
    my_row = pl.multiple_of(lax.axis_index("pair") * ROWS, ROWS)
    nblk = table_ref.shape[1] // BS

    rows_ref[...] = jnp.zeros_like(rows_ref)
    for t in range(FAR):
        block = jnp.clip(own_first - 2 + t, 0, nblk - 1)
        values = table_ref[:, pl.ds(pl.multiple_of(block * BS, BS), BS)]
        rows_ref[t : t + 1, :] = values[0:1, :]
        rows_ref[8 + t : 9 + t, :] = 2.0 * block.astype(jnp.float32) + values[1:2, :]
        for p in range(NAUX):
            rows_ref[16 + 8 * p + t : 17 + 8 * p + t, :] = values[2 + p : 3 + p, :]
    cols_ref[...] = rows_ref[...].T

    def tiles(columns, t_row, t_col):
        def column(quantity):
            at = 8 * quantity + t_row
            return columns[:, at : at + 1]

        def row(quantity):
            at = 8 * quantity + t_col
            return rows_ref[at : at + 1, :]

        e_r, e_c = column(0), row(0)
        reduced = e_r * e_c / (e_r + e_c)
        distance = column(1) - row(1)
        overlap = jnp.exp(-reduced * distance * distance)
        return [
            (overlap * jnp.tanh(column(2 + p) * row(2 + p))).astype(jnp.bfloat16)
            for p in range(NAUX)
        ]

    step = 32
    for t_far in range(FAR):
        for start in range(0, BS, step):
            columns = cols_ref[start : start + step, :]
            for near in range(NEAR):
                side = t_far - near
                if 0 <= side <= 2:
                    for p, tile in enumerate(tiles(columns, t_far, near + 1)):
                        at = (side * NAUX + p) * BS + start
                        right_ref[near, at : at + step, :] = tile

    mine = cols_ref[pl.ds(my_row, ROWS), :]
    for at, (near, own) in enumerate(LEFT_PAIRS):
        made = tiles(mine, own + 2, near + 1)
        left_ref[at * 32 : at * 32 + 32, :] = jnp.concatenate(made, axis=0)


def products_kernel(bank_ref, right_ref, left_ref, out_ref, half_ref, times_ref, mixed_ref):
    def bank(tile):
        return bank_ref[:, tile].astype(jnp.float32).reshape(BS, BS)

    own_first = lax.axis_index("blk") * OWN
    slot = lax.broadcasted_iota(jnp.int32, (1, BS), 1)
    code_row = lax.broadcasted_iota(jnp.int32, (BS, BS), 0)
    lists = bank_ref[:, NEAR * BAND].astype(jnp.float32).astype(jnp.int32)
    found = jnp.zeros((BS, BS), jnp.float32)
    for q in range(lists.shape[0]):
        row_b, col_b, mid_b, far_b = (lists[q, n : n + 1, :] for n in range(4))
        length = lists[q, 4:5, 0:1]
        code = (
            (row_b - own_first) * 27 + (col_b - row_b + 1) * 9 + (mid_b - row_b + 1) * 3 + far_b - mid_b + 1
        )
        code = jnp.where(slot < length, code, BS)
        found += (code == code_row).astype(jnp.float32)
    times_ref[...] = jnp.dot(
        found.astype(jnp.bfloat16), jnp.ones((BS, BS), jnp.bfloat16), preferred_element_type=jnp.float32
    )

    for near in range(NEAR):
        density = jnp.concatenate([bank(near * BAND + c) for c in range(BAND)], axis=1)
        density = density.astype(jnp.bfloat16)
        owners = owners_of(near)
        at = FIRST_LEFT[(near, owners[0])] * 32
        size = len(owners) * 32
        half = jnp.dot(left_ref[at : at + size, :], density, preferred_element_type=jnp.float32)
        half_ref[at : at + size, :] = half.astype(jnp.bfloat16).astype(jnp.float32)

    for j in range(NEAR):
        owners = owners_of(j)
        for slot, i in enumerate(owners):
            for side in range(3):
                far = j - 1 + side
                total = [None] * NAUX
                for k in range(i, i + 3):
                    if abs(far - k) > 1:
                        continue
                    code = i * 27 + (j - i) * 9 + (k - i) * 3 + far - k + 1
                    times = times_ref[code : code + 1, :]
                    at = FIRST_LEFT[(k, i)] * 32
                    column = (far - k + 1) * BS
                    for p in range(NAUX):
                        piece = times * half_ref[
                            at + p * ROWS : at + (p + 1) * ROWS, column : column + BS
                        ]
                        total[p] = piece if total[p] is None else total[p] + piece
                for p in range(NAUX):
                    high = total[p].astype(jnp.bfloat16)
                    low = total[p] - high.astype(jnp.float32)
                    both = jnp.concatenate([high.astype(jnp.float32), low], axis=0)
                    column = (side * NAUX + p) * BS
                    mixed_ref[slot * 16 : slot * 16 + 16, column : column + BS] = both.astype(
                        jnp.bfloat16
                    )
        size = len(owners) * 16
        term = jnp.dot(mixed_ref[:size, :], right_ref[j], preferred_element_type=jnp.float32)
        for slot, i in enumerate(owners):
            pair = term[slot * 16 : slot * 16 + 8] + term[slot * 16 + 8 : slot * 16 + 16]
            out_ref[i, j - i] = pair * SCALE


def vmem(count):
    return [pl.BlockSpec(memory_space=pltpu.VMEM)] * count


def shards(density, exponents, offsets, expansion, quartet_list, list_length):
    count = lax.axis_size("blk")
    odd = (lax.axis_index("blk") & 1) == 1

    def exchanged(first):
        lower = range(first, count - 1, 2)
        return lax.ppermute(density, "blk", [(i, i + 1) for i in lower] + [(i + 1, i) for i in lower])

    inner, outer = exchanged(0), exchanged(1)
    low = jnp.where(odd, inner[OWN - 1], outer[OWN - 1])
    high = jnp.where(odd, outer[0], inner[0])

    tables = jnp.concatenate([exponents[None], offsets[None], expansion], axis=0)
    right, left = pl.pallas_call(
        factors_kernel,
        out_shape=(
            jax.ShapeDtypeStruct((NEAR, 3 * NAUX * BS, BS), jnp.bfloat16),
            jax.ShapeDtypeStruct((len(LEFT_PAIRS) * NAUX * ROWS, BS), jnp.bfloat16),
        ),
        in_specs=vmem(1),
        out_specs=tuple(vmem(2)),
        scratch_shapes=[pltpu.VMEM((BS, BS), jnp.float32), pltpu.VMEM((BS, BS), jnp.float32)],
        compiler_params=pltpu.CompilerParams(vmem_limit_bytes=24 * 2**20),
        cost_estimate=pl.CostEstimate(flops=30_000_000, bytes_accessed=3_000_000, transcendentals=1_500_000),
        name="factors",
    )(tables)

    listed = jnp.pad(quartet_list[0, 0], ((0, ROWS - 4), (0, 0)))
    listed += jnp.pad(list_length, ((4, ROWS - 5), (0, BS - 1)))
    payload = jnp.concatenate(
        [low, density.reshape(OWN * BAND, ROWS, BS), high, listed.astype(jnp.bfloat16)[None]], axis=0
    )
    bank = lax.all_gather(payload, "pair", axis=0)

    return pl.pallas_call(
        products_kernel,
        out_shape=jax.ShapeDtypeStruct((OWN, BAND, ROWS, BS), jnp.float32),
        in_specs=vmem(3),
        out_specs=pl.BlockSpec(memory_space=pltpu.VMEM),
        scratch_shapes=[
            pltpu.VMEM((len(LEFT_PAIRS) * NAUX * ROWS, BAND * BS), jnp.float32),
            pltpu.VMEM((BS, BS), jnp.float32),
            pltpu.VMEM((3 * 16, 3 * NAUX * BS), jnp.bfloat16),
        ],
        compiler_params=pltpu.CompilerParams(vmem_limit_bytes=24 * 2**20),
        name="products",
    )(bank, right, left)


def solution(mesh):
    return jax.shard_map(
        shards,
        mesh=mesh,
        in_specs=(
            P("blk", None, "pair", None),
            P(),
            P(),
            P(),
            P("blk", "pair", None, None),
            P("blk", "pair"),
        ),
        out_specs=P("blk", None, "pair", None),
        check_vma=False,
    )
```

```python
import jax
import jax.numpy as jnp
from jax import lax
from jax.experimental import pallas as pl
from jax.experimental.pallas import tpu as pltpu
from jax.sharding import PartitionSpec as P

BS = 128
NAUX = 4
OWN = 3
BAND = 3
NEAR = OWN + 2
FAR = OWN + 4
ROWS = 8
SCALE = 0.0078125

LEFT_PAIRS = [(k, i) for k in range(NEAR) for i in range(OWN) if abs(i - (k - 1)) <= 1]
FIRST_LEFT = {pair: at for at, pair in enumerate(LEFT_PAIRS)}


def owners_of(near):
    return [i for i in range(OWN) if abs(i - (near - 1)) <= 1]


def early():
    return lax.axis_index("pair") < 4


def make_factors(table_ref, right_ref, left_ref, rows_ref, cols_ref):
    own_first = lax.axis_index("blk") * OWN
    my_row = pl.multiple_of(lax.axis_index("pair") * ROWS, ROWS)
    nblk = table_ref.shape[1] // BS

    rows_ref[...] = jnp.zeros_like(rows_ref)
    for t in range(FAR):
        block = jnp.clip(own_first - 2 + t, 0, nblk - 1)
        values = table_ref[:, pl.ds(pl.multiple_of(block * BS, BS), BS)]
        rows_ref[t : t + 1, :] = values[0:1, :]
        rows_ref[8 + t : 9 + t, :] = 2.0 * block.astype(jnp.float32) + values[1:2, :]
        for p in range(NAUX):
            rows_ref[16 + 8 * p + t : 17 + 8 * p + t, :] = values[2 + p : 3 + p, :]
    cols_ref[...] = rows_ref[...].T

    def tiles(columns, t_row, t_col):
        def column(quantity):
            at = 8 * quantity + t_row
            return columns[:, at : at + 1]

        def row(quantity):
            at = 8 * quantity + t_col
            return rows_ref[at : at + 1, :]

        e_r, e_c = column(0), row(0)
        reduced = e_r * e_c / (e_r + e_c)
        distance = column(1) - row(1)
        overlap = jnp.exp(-reduced * distance * distance)
        return [
            (overlap * jnp.tanh(column(2 + p) * row(2 + p))).astype(jnp.bfloat16)
            for p in range(NAUX)
        ]

    step = 32
    for t_far in range(FAR):
        for start in range(0, BS, step):
            columns = cols_ref[start : start + step, :]
            for near in range(NEAR):
                side = t_far - near
                if 0 <= side <= 2:
                    for p, tile in enumerate(tiles(columns, t_far, near + 1)):
                        at = (side * NAUX + p) * BS + start
                        right_ref[near, at : at + step, :] = tile

    mine = cols_ref[pl.ds(my_row, ROWS), :]
    for at, (near, own) in enumerate(LEFT_PAIRS):
        made = tiles(mine, own + 2, near + 1)
        left_ref[at * 32 : at * 32 + 32, :] = jnp.concatenate(made, axis=0)


def factors_kernel(table_ref, right_ref, left_ref, rows_ref, cols_ref):
    @pl.when(early())
    def _():
        make_factors(table_ref, right_ref, left_ref, rows_ref, cols_ref)


def products_kernel(
    bank_ref, table_ref, right_in, left_in, out_ref,
    half_ref, times_ref, mixed_ref, right_ref, left_ref, rows_ref, cols_ref
):
    @pl.when(early())
    def _():
        make_products(bank_ref, right_in, left_in, out_ref, half_ref, times_ref, mixed_ref)

    @pl.when(jnp.logical_not(early()))
    def _():
        make_factors(table_ref, right_ref, left_ref, rows_ref, cols_ref)
        make_products(bank_ref, right_ref, left_ref, out_ref, half_ref, times_ref, mixed_ref)


def make_products(bank_ref, right_ref, left_ref, out_ref, half_ref, times_ref, mixed_ref):
    def bank(tile):
        return bank_ref[:, tile].astype(jnp.float32).reshape(BS, BS)

    own_first = lax.axis_index("blk") * OWN
    slot = lax.broadcasted_iota(jnp.int32, (1, BS), 1)
    code_row = lax.broadcasted_iota(jnp.int32, (BS, BS), 0)
    lists = bank_ref[:, NEAR * BAND].astype(jnp.float32).astype(jnp.int32)
    found = jnp.zeros((BS, BS), jnp.float32)
    for q in range(lists.shape[0]):
        row_b, col_b, mid_b, far_b = (lists[q, n : n + 1, :] for n in range(4))
        length = lists[q, 4:5, 0:1]
        code = (
            (row_b - own_first) * 27 + (col_b - row_b + 1) * 9 + (mid_b - row_b + 1) * 3 + far_b - mid_b + 1
        )
        code = jnp.where(slot < length, code, BS)
        found += (code == code_row).astype(jnp.float32)
    times_ref[...] = jnp.dot(
        found.astype(jnp.bfloat16), jnp.ones((BS, BS), jnp.bfloat16), preferred_element_type=jnp.float32
    )

    for near in range(NEAR):
        density = jnp.concatenate([bank(near * BAND + c) for c in range(BAND)], axis=1)
        density = density.astype(jnp.bfloat16)
        owners = owners_of(near)
        at = FIRST_LEFT[(near, owners[0])] * 32
        size = len(owners) * 32
        half = jnp.dot(left_ref[at : at + size, :], density, preferred_element_type=jnp.float32)
        half_ref[at : at + size, :] = half.astype(jnp.bfloat16).astype(jnp.float32)

    for j in range(NEAR):
        owners = owners_of(j)
        for slot, i in enumerate(owners):
            for side in range(3):
                far = j - 1 + side
                total = [None] * NAUX
                for k in range(i, i + 3):
                    if abs(far - k) > 1:
                        continue
                    code = i * 27 + (j - i) * 9 + (k - i) * 3 + far - k + 1
                    times = times_ref[code : code + 1, :]
                    at = FIRST_LEFT[(k, i)] * 32
                    column = (far - k + 1) * BS
                    for p in range(NAUX):
                        piece = times * half_ref[
                            at + p * ROWS : at + (p + 1) * ROWS, column : column + BS
                        ]
                        total[p] = piece if total[p] is None else total[p] + piece
                for p in range(NAUX):
                    high = total[p].astype(jnp.bfloat16)
                    low = total[p] - high.astype(jnp.float32)
                    both = jnp.concatenate([high.astype(jnp.float32), low], axis=0)
                    column = (side * NAUX + p) * BS
                    mixed_ref[slot * 16 : slot * 16 + 16, column : column + BS] = both.astype(
                        jnp.bfloat16
                    )
        size = len(owners) * 16
        term = jnp.dot(mixed_ref[:size, :], right_ref[j], preferred_element_type=jnp.float32)
        for slot, i in enumerate(owners):
            pair = term[slot * 16 : slot * 16 + 8] + term[slot * 16 + 8 : slot * 16 + 16]
            out_ref[i, j - i] = pair * SCALE


def vmem(count):
    return [pl.BlockSpec(memory_space=pltpu.VMEM)] * count


def shards(density, exponents, offsets, expansion, quartet_list, list_length):
    count = lax.axis_size("blk")
    forward = [(i, i + 1) for i in range(count - 1)]
    backward = [(i + 1, i) for i in range(count - 1)]
    low = lax.ppermute(density, "blk", forward)[OWN - 1]
    high = lax.ppermute(density, "blk", backward)[0]

    tables = jnp.concatenate([exponents[None], offsets[None], expansion], axis=0)
    right, left = pl.pallas_call(
        factors_kernel,
        out_shape=(
            jax.ShapeDtypeStruct((NEAR, 3 * NAUX * BS, BS), jnp.bfloat16),
            jax.ShapeDtypeStruct((len(LEFT_PAIRS) * NAUX * ROWS, BS), jnp.bfloat16),
        ),
        in_specs=vmem(1),
        out_specs=tuple(vmem(2)),
        scratch_shapes=[pltpu.VMEM((BS, BS), jnp.float32), pltpu.VMEM((BS, BS), jnp.float32)],
        compiler_params=pltpu.CompilerParams(vmem_limit_bytes=24 * 2**20),
        cost_estimate=pl.CostEstimate(flops=30_000_000, bytes_accessed=3_000_000, transcendentals=1_500_000),
        name="factors",
    )(tables)

    listed = jnp.pad(quartet_list[0, 0], ((0, ROWS - 4), (0, 0)))
    listed += jnp.pad(list_length, ((4, ROWS - 5), (0, BS - 1)))
    payload = jnp.concatenate(
        [low, density.reshape(OWN * BAND, ROWS, BS), high, listed.astype(jnp.bfloat16)[None]], axis=0
    )
    payload, right, left = lax.optimization_barrier((payload, right, left))
    bank = lax.all_gather(payload, "pair", axis=0)

    return pl.pallas_call(
        products_kernel,
        out_shape=jax.ShapeDtypeStruct((OWN, BAND, ROWS, BS), jnp.float32),
        in_specs=vmem(4),
        out_specs=pl.BlockSpec(memory_space=pltpu.VMEM),
        scratch_shapes=[
            pltpu.VMEM((len(LEFT_PAIRS) * NAUX * ROWS, BAND * BS), jnp.float32),
            pltpu.VMEM((BS, BS), jnp.float32),
            pltpu.VMEM((3 * 16, 3 * NAUX * BS), jnp.bfloat16),
            pltpu.VMEM(right.shape, jnp.bfloat16),
            pltpu.VMEM(left.shape, jnp.bfloat16),
            pltpu.VMEM((BS, BS), jnp.float32),
            pltpu.VMEM((BS, BS), jnp.float32),
        ],
        compiler_params=pltpu.CompilerParams(vmem_limit_bytes=24 * 2**20),
        name="products",
    )(bank, tables, right, left)


def solution(mesh):
    return jax.shard_map(
        shards,
        mesh=mesh,
        in_specs=(
            P("blk", None, "pair", None),
            P(),
            P(),
            P(),
            P("blk", "pair", None, None),
            P("blk", "pair"),
        ),
        out_specs=P("blk", None, "pair", None),
        check_vma=False,
    )
```

```python
import jax
import jax.numpy as jnp
from jax import lax
from jax.experimental import pallas as pl
from jax.experimental.pallas import tpu as pltpu
from jax.sharding import PartitionSpec as P

BS = 128
NAUX = 4
OWN = 3
BAND = 3
NEAR = OWN + 2
FAR = OWN + 4
ROWS = 8
SCALE = 0.0078125

LEFT_PAIRS = [(k, i) for k in range(NEAR) for i in range(OWN) if abs(i - (k - 1)) <= 1]
FIRST_LEFT = {pair: at for at, pair in enumerate(LEFT_PAIRS)}


def owners_of(near):
    return [i for i in range(OWN) if abs(i - (near - 1)) <= 1]


def early():
    return lax.axis_index("pair") < 4


def make_factors(table_ref, right_ref, left_ref, rows_ref, cols_ref):
    own_first = lax.axis_index("blk") * OWN
    my_row = pl.multiple_of(lax.axis_index("pair") * ROWS, ROWS)
    nblk = table_ref.shape[1] // BS

    rows_ref[...] = jnp.zeros_like(rows_ref)
    for t in range(FAR):
        block = jnp.clip(own_first - 2 + t, 0, nblk - 1)
        values = table_ref[:, pl.ds(pl.multiple_of(block * BS, BS), BS)]
        rows_ref[t : t + 1, :] = values[0:1, :]
        rows_ref[8 + t : 9 + t, :] = 2.0 * block.astype(jnp.float32) + values[1:2, :]
        for p in range(NAUX):
            rows_ref[16 + 8 * p + t : 17 + 8 * p + t, :] = values[2 + p : 3 + p, :]
    cols_ref[...] = rows_ref[...].T

    def tiles(columns, t_row, t_col):
        def column(quantity):
            at = 8 * quantity + t_row
            return columns[:, at : at + 1]

        def row(quantity):
            at = 8 * quantity + t_col
            return rows_ref[at : at + 1, :]

        e_r, e_c = column(0), row(0)
        reduced = e_r * e_c / (e_r + e_c)
        distance = column(1) - row(1)
        overlap = jnp.exp(-reduced * distance * distance)
        return [
            (overlap * jnp.tanh(column(2 + p) * row(2 + p))).astype(jnp.bfloat16)
            for p in range(NAUX)
        ]

    step = 32
    for t_far in range(FAR):
        for start in range(0, BS, step):
            columns = cols_ref[start : start + step, :]
            for near in range(NEAR):
                side = t_far - near
                if 0 <= side <= 2:
                    for p, tile in enumerate(tiles(columns, t_far, near + 1)):
                        at = (side * NAUX + p) * BS + start
                        right_ref[near, at : at + step, :] = tile

    mine = cols_ref[pl.ds(my_row, ROWS), :]
    for at, (near, own) in enumerate(LEFT_PAIRS):
        made = tiles(mine, own + 2, near + 1)
        left_ref[at * 32 : at * 32 + 32, :] = jnp.concatenate(made, axis=0)


def factors_kernel(table_ref, right_ref, left_ref, rows_ref, cols_ref):
    @pl.when(early())
    def _():
        make_factors(table_ref, right_ref, left_ref, rows_ref, cols_ref)


def products_kernel(
    bank_ref, table_ref, right_in, left_in, out_ref,
    half_ref, times_ref, mixed_ref, right_ref, left_ref, rows_ref, cols_ref
):
    @pl.when(early())
    def _():
        make_products(bank_ref, right_in, left_in, out_ref, half_ref, times_ref, mixed_ref)

    @pl.when(jnp.logical_not(early()))
    def _():
        make_factors(table_ref, right_ref, left_ref, rows_ref, cols_ref)
        make_products(bank_ref, right_ref, left_ref, out_ref, half_ref, times_ref, mixed_ref)


def make_products(bank_ref, right_ref, left_ref, out_ref, half_ref, times_ref, mixed_ref):
    devices = bank_ref.shape[0]

    def bank(near, c):
        if 0 < near < NEAR - 1:
            pieces = [bank_ref[q, (near - 1) * BAND + c] for q in range(devices)]
        else:
            holder = 0 if near == 0 else 1
            pieces = [bank_ref[q // 2 * 2 + holder, OWN * BAND + 2 * c + q % 2] for q in range(devices)]
        return jnp.concatenate([piece.astype(jnp.float32) for piece in pieces], axis=0)

    own_first = lax.axis_index("blk") * OWN
    slot = lax.broadcasted_iota(jnp.int32, (1, BS), 1)
    code_row = lax.broadcasted_iota(jnp.int32, (BS, BS), 0)
    lists = bank_ref[:, NEAR * BAND].astype(jnp.float32).astype(jnp.int32)
    found = jnp.zeros((BS, BS), jnp.float32)
    for q in range(lists.shape[0]):
        row_b, col_b, mid_b, far_b = (lists[q, n : n + 1, :] for n in range(4))
        length = lists[q, 4:5, 0:1]
        code = (
            (row_b - own_first) * 27 + (col_b - row_b + 1) * 9 + (mid_b - row_b + 1) * 3 + far_b - mid_b + 1
        )
        code = jnp.where(slot < length, code, BS)
        found += (code == code_row).astype(jnp.float32)
    times_ref[...] = jnp.dot(
        found.astype(jnp.bfloat16), jnp.ones((BS, BS), jnp.bfloat16), preferred_element_type=jnp.float32
    )

    for near in range(NEAR):
        density = jnp.concatenate([bank(near, c) for c in range(BAND)], axis=1)
        density = density.astype(jnp.bfloat16)
        owners = owners_of(near)
        at = FIRST_LEFT[(near, owners[0])] * 32
        size = len(owners) * 32
        half = jnp.dot(left_ref[at : at + size, :], density, preferred_element_type=jnp.float32)
        half_ref[at : at + size, :] = half.astype(jnp.bfloat16).astype(jnp.float32)

    for j in range(NEAR):
        owners = owners_of(j)
        for slot, i in enumerate(owners):
            for side in range(3):
                far = j - 1 + side
                total = [None] * NAUX
                for k in range(i, i + 3):
                    if abs(far - k) > 1:
                        continue
                    code = i * 27 + (j - i) * 9 + (k - i) * 3 + far - k + 1
                    times = times_ref[code : code + 1, :]
                    at = FIRST_LEFT[(k, i)] * 32
                    column = (far - k + 1) * BS
                    for p in range(NAUX):
                        piece = times * half_ref[
                            at + p * ROWS : at + (p + 1) * ROWS, column : column + BS
                        ]
                        total[p] = piece if total[p] is None else total[p] + piece
                for p in range(NAUX):
                    high = total[p].astype(jnp.bfloat16)
                    low = total[p] - high.astype(jnp.float32)
                    both = jnp.concatenate([high.astype(jnp.float32), low], axis=0)
                    column = (side * NAUX + p) * BS
                    mixed_ref[slot * 16 : slot * 16 + 16, column : column + BS] = both.astype(
                        jnp.bfloat16
                    )
        size = len(owners) * 16
        term = jnp.dot(mixed_ref[:size, :], right_ref[j], preferred_element_type=jnp.float32)
        for slot, i in enumerate(owners):
            pair = term[slot * 16 : slot * 16 + 8] + term[slot * 16 + 8 : slot * 16 + 16]
            out_ref[i, j - i] = pair * SCALE


def vmem(count):
    return [pl.BlockSpec(memory_space=pltpu.VMEM)] * count


def shards(density, exponents, offsets, expansion, quartet_list, list_length):
    count = lax.axis_size("blk")
    pairs = lax.axis_size("pair")
    second = (lax.axis_index("pair") & 1) == 1

    other = lax.ppermute(density, "pair", [(q, q ^ 1) for q in range(pairs)])
    facing = jnp.where(
        second,
        jnp.stack([other[OWN - 1], density[OWN - 1]], axis=1),
        jnp.stack([density[0], other[0]], axis=1),
    )
    facing, exponents, quartet_list = lax.optimization_barrier((facing, exponents, quartet_list))
    ups = [(b * pairs + q, (b + 1) * pairs + q - 1) for b in range(count - 1) for q in range(1, pairs, 2)]
    halo = lax.ppermute(facing, ("blk", "pair"), ups + [(high, low) for low, high in ups])

    tables = jnp.concatenate([exponents[None], offsets[None], expansion], axis=0)
    right, left = pl.pallas_call(
        factors_kernel,
        out_shape=(
            jax.ShapeDtypeStruct((NEAR, 3 * NAUX * BS, BS), jnp.bfloat16),
            jax.ShapeDtypeStruct((len(LEFT_PAIRS) * NAUX * ROWS, BS), jnp.bfloat16),
        ),
        in_specs=vmem(1),
        out_specs=tuple(vmem(2)),
        scratch_shapes=[pltpu.VMEM((BS, BS), jnp.float32), pltpu.VMEM((BS, BS), jnp.float32)],
        compiler_params=pltpu.CompilerParams(vmem_limit_bytes=24 * 2**20),
        cost_estimate=pl.CostEstimate(flops=30_000_000, bytes_accessed=3_000_000, transcendentals=1_500_000),
        name="factors",
    )(tables)

    listed = jnp.pad(quartet_list[0, 0], ((0, ROWS - 4), (0, 0)))
    listed += jnp.pad(list_length, ((4, ROWS - 5), (0, BS - 1)))
    payload = jnp.concatenate(
        [
            density.reshape(OWN * BAND, ROWS, BS),
            halo.reshape(BAND * 2, ROWS, BS),
            listed.astype(jnp.bfloat16)[None],
        ],
        axis=0,
    )
    payload, right, left = lax.optimization_barrier((payload, right, left))
    bank = lax.all_gather(payload, "pair", axis=0)

    return pl.pallas_call(
        products_kernel,
        out_shape=jax.ShapeDtypeStruct((OWN, BAND, ROWS, BS), jnp.float32),
        in_specs=vmem(4),
        out_specs=pl.BlockSpec(memory_space=pltpu.VMEM),
        scratch_shapes=[
            pltpu.VMEM((len(LEFT_PAIRS) * NAUX * ROWS, BAND * BS), jnp.float32),
            pltpu.VMEM((BS, BS), jnp.float32),
            pltpu.VMEM((3 * 16, 3 * NAUX * BS), jnp.bfloat16),
            pltpu.VMEM(right.shape, jnp.bfloat16),
            pltpu.VMEM(left.shape, jnp.bfloat16),
            pltpu.VMEM((BS, BS), jnp.float32),
            pltpu.VMEM((BS, BS), jnp.float32),
        ],
        compiler_params=pltpu.CompilerParams(vmem_limit_bytes=24 * 2**20),
        name="products",
    )(bank, tables, right, left)


def solution(mesh):
    return jax.shard_map(
        shards,
        mesh=mesh,
        in_specs=(
            P("blk", None, "pair", None),
            P(),
            P(),
            P(),
            P("blk", "pair", None, None),
            P("blk", "pair"),
        ),
        out_specs=P("blk", None, "pair", None),
        check_vma=False,
    )
```

```python
import jax
import jax.numpy as jnp
from jax import lax
from jax.experimental import pallas as pl
from jax.experimental.pallas import tpu as pltpu
from jax.sharding import PartitionSpec as P

BS = 128
NAUX = 4
OWN = 3
BAND = 3
NEAR = OWN + 2
FAR = OWN + 4
ROWS = 8
SCALE = 0.0078125
OWN_ROWS = (OWN * BAND + 1) * ROWS

LEFT_PAIRS = [(k, i) for k in range(NEAR) for i in range(OWN) if abs(i - (k - 1)) <= 1]
FIRST_LEFT = {pair: at for at, pair in enumerate(LEFT_PAIRS)}


def owners_of(near):
    return [i for i in range(OWN) if abs(i - (near - 1)) <= 1]


def early():
    return lax.axis_index("pair") < 4


def make_factors(table_ref, right_ref, left_ref, rows_ref, cols_ref):
    own_first = lax.axis_index("blk") * OWN
    my_row = pl.multiple_of(lax.axis_index("pair") * ROWS, ROWS)
    nblk = (table_ref.shape[0] - OWN_ROWS) // (2 + NAUX)

    rows_ref[...] = jnp.zeros_like(rows_ref)
    for t in range(FAR):
        block = jnp.clip(own_first - 2 + t, 0, nblk - 1)
        rows_ref[t : t + 1, :] = table_ref[pl.ds(block, 1), :]
        offset = table_ref[pl.ds(nblk + block, 1), :]
        rows_ref[8 + t : 9 + t, :] = 2.0 * block.astype(jnp.float32) + offset
        for p in range(NAUX):
            weight = table_ref[pl.ds(2 * nblk + NAUX * block + p, 1), :]
            rows_ref[16 + 8 * p + t : 17 + 8 * p + t, :] = weight
    cols_ref[...] = rows_ref[...].T

    def tiles(columns, t_row, t_col):
        def column(quantity):
            at = 8 * quantity + t_row
            return columns[:, at : at + 1]

        def row(quantity):
            at = 8 * quantity + t_col
            return rows_ref[at : at + 1, :]

        e_r, e_c = column(0), row(0)
        reduced = e_r * e_c / (e_r + e_c)
        distance = column(1) - row(1)
        overlap = jnp.exp(-reduced * distance * distance)
        return [
            (overlap * jnp.tanh(column(2 + p) * row(2 + p))).astype(jnp.bfloat16)
            for p in range(NAUX)
        ]

    step = 32
    for t_far in range(FAR):
        for start in range(0, BS, step):
            columns = cols_ref[start : start + step, :]
            for near in range(NEAR):
                side = t_far - near
                if 0 <= side <= 2:
                    for p, tile in enumerate(tiles(columns, t_far, near + 1)):
                        at = (side * NAUX + p) * BS + start
                        right_ref[near, at : at + step, :] = tile

    mine = cols_ref[pl.ds(my_row, ROWS), :]
    for at, (near, own) in enumerate(LEFT_PAIRS):
        made = tiles(mine, own + 2, near + 1)
        left_ref[at * 32 : at * 32 + 32, :] = jnp.concatenate(made, axis=0)


def factors_kernel(table_ref, right_ref, left_ref, rows_ref, cols_ref):
    @pl.when(early())
    def _():
        make_factors(table_ref, right_ref, left_ref, rows_ref, cols_ref)


def products_kernel(
    bank_ref, table_ref, right_in, left_in, out_ref,
    half_ref, times_ref, mixed_ref, right_ref, left_ref, rows_ref, cols_ref
):
    @pl.when(early())
    def _():
        make_products(bank_ref, right_in, left_in, out_ref, half_ref, times_ref, mixed_ref)

    @pl.when(jnp.logical_not(early()))
    def _():
        make_factors(table_ref, right_ref, left_ref, rows_ref, cols_ref)
        make_products(bank_ref, right_ref, left_ref, out_ref, half_ref, times_ref, mixed_ref)


def make_products(bank_ref, right_ref, left_ref, out_ref, half_ref, times_ref, mixed_ref):
    devices = bank_ref.shape[0]

    def bank(near, c):
        if 0 < near < NEAR - 1:
            pieces = [bank_ref[q, (near - 1) * BAND + c] for q in range(devices)]
        else:
            holder = 0 if near == 0 else 1
            pieces = [bank_ref[q // 2 * 2 + holder, OWN * BAND + 1 + 2 * c + q % 2] for q in range(devices)]
        return jnp.concatenate([piece.astype(jnp.float32) for piece in pieces], axis=0)

    own_first = lax.axis_index("blk") * OWN
    slot = lax.broadcasted_iota(jnp.int32, (1, BS), 1)
    code_row = lax.broadcasted_iota(jnp.int32, (BS, BS), 0)
    lists = bank_ref[:, OWN * BAND].astype(jnp.float32).astype(jnp.int32)
    found = jnp.zeros((BS, BS), jnp.float32)
    for q in range(lists.shape[0]):
        row_b, col_b, mid_b, far_b = (lists[q, n : n + 1, :] for n in range(4))
        length = lists[q, 4:5, 0:1]
        code = (
            (row_b - own_first) * 27 + (col_b - row_b + 1) * 9 + (mid_b - row_b + 1) * 3 + far_b - mid_b + 1
        )
        code = jnp.where(slot < length, code, BS)
        found += (code == code_row).astype(jnp.float32)
    times_ref[...] = jnp.dot(
        found.astype(jnp.bfloat16), jnp.ones((BS, BS), jnp.bfloat16), preferred_element_type=jnp.float32
    )

    for near in range(NEAR):
        density = jnp.concatenate([bank(near, c) for c in range(BAND)], axis=1)
        density = density.astype(jnp.bfloat16)
        owners = owners_of(near)
        at = FIRST_LEFT[(near, owners[0])] * 32
        size = len(owners) * 32
        half = jnp.dot(left_ref[at : at + size, :], density, preferred_element_type=jnp.float32)
        half_ref[at : at + size, :] = half.astype(jnp.bfloat16).astype(jnp.float32)

    for j in range(NEAR):
        owners = owners_of(j)
        for slot, i in enumerate(owners):
            for side in range(3):
                far = j - 1 + side
                total = [None] * NAUX
                for k in range(i, i + 3):
                    if abs(far - k) > 1:
                        continue
                    code = i * 27 + (j - i) * 9 + (k - i) * 3 + far - k + 1
                    times = times_ref[code : code + 1, :]
                    at = FIRST_LEFT[(k, i)] * 32
                    column = (far - k + 1) * BS
                    for p in range(NAUX):
                        piece = times * half_ref[
                            at + p * ROWS : at + (p + 1) * ROWS, column : column + BS
                        ]
                        total[p] = piece if total[p] is None else total[p] + piece
                for p in range(NAUX):
                    high = total[p].astype(jnp.bfloat16)
                    low = total[p] - high.astype(jnp.float32)
                    both = jnp.concatenate([high.astype(jnp.float32), low], axis=0)
                    column = (side * NAUX + p) * BS
                    mixed_ref[slot * 16 : slot * 16 + 16, column : column + BS] = both.astype(
                        jnp.bfloat16
                    )
        size = len(owners) * 16
        term = jnp.dot(mixed_ref[:size, :], right_ref[j], preferred_element_type=jnp.float32)
        for slot, i in enumerate(owners):
            pair = term[slot * 16 : slot * 16 + 8] + term[slot * 16 + 8 : slot * 16 + 16]
            out_ref[i, j - i] = pair * SCALE


def vmem(count):
    return [pl.BlockSpec(memory_space=pltpu.VMEM)] * count


def shards(density, exponents, offsets, expansion, quartet_list, list_length):
    count = lax.axis_size("blk")
    pairs = lax.axis_size("pair")
    second = (lax.axis_index("pair") & 1) == 1

    other = lax.ppermute(density, "pair", [(q, q ^ 1) for q in range(pairs)])

    nblk = exponents.shape[0] // BS
    pieces = [
        exponents.reshape(nblk, BS),
        offsets.reshape(nblk, BS),
        expansion.reshape(NAUX, nblk, BS).transpose(1, 0, 2).reshape(NAUX * nblk, BS),
        density.reshape(OWN * BAND * ROWS, BS),
        quartet_list[0, 0],
        list_length,
    ]
    rows, tables, at = (2 + NAUX) * nblk + OWN_ROWS, 0.0, 0
    for piece in pieces:
        high, wide = piece.shape
        tables += jnp.pad(piece, ((at, rows - at - high), (0, BS - wide))).astype(jnp.float32)
        at += high
    tables = lax.optimization_barrier(tables)
    own = tables[-OWN_ROWS:].astype(jnp.bfloat16).reshape(OWN * BAND + 1, ROWS, BS)
    facing = jnp.where(
        second,
        jnp.stack([other[OWN - 1], own[(OWN - 1) * BAND : OWN * BAND]], axis=1),
        jnp.stack([own[:BAND], other[0]], axis=1),
    )
    ups = [(b * pairs + q, (b + 1) * pairs + q - 1) for b in range(count - 1) for q in range(1, pairs, 2)]
    halo = lax.ppermute(facing, ("blk", "pair"), ups + [(high, low) for low, high in ups])

    right, left = pl.pallas_call(
        factors_kernel,
        out_shape=(
            jax.ShapeDtypeStruct((NEAR, 3 * NAUX * BS, BS), jnp.bfloat16),
            jax.ShapeDtypeStruct((len(LEFT_PAIRS) * NAUX * ROWS, BS), jnp.bfloat16),
        ),
        in_specs=vmem(1),
        out_specs=tuple(vmem(2)),
        scratch_shapes=[pltpu.VMEM((BS, BS), jnp.float32), pltpu.VMEM((BS, BS), jnp.float32)],
        compiler_params=pltpu.CompilerParams(vmem_limit_bytes=24 * 2**20),
        cost_estimate=pl.CostEstimate(flops=30_000_000, bytes_accessed=3_000_000, transcendentals=1_500_000),
        name="factors",
    )(tables)

    payload = jnp.concatenate([own, halo.reshape(BAND * 2, ROWS, BS)], axis=0)
    payload, right, left = lax.optimization_barrier((payload, right, left))
    bank = lax.all_gather(payload, "pair", axis=0)

    return pl.pallas_call(
        products_kernel,
        out_shape=jax.ShapeDtypeStruct((OWN, BAND, ROWS, BS), jnp.float32),
        in_specs=vmem(4),
        out_specs=pl.BlockSpec(memory_space=pltpu.VMEM),
        scratch_shapes=[
            pltpu.VMEM((len(LEFT_PAIRS) * NAUX * ROWS, BAND * BS), jnp.float32),
            pltpu.VMEM((BS, BS), jnp.float32),
            pltpu.VMEM((3 * 16, 3 * NAUX * BS), jnp.bfloat16),
            pltpu.VMEM(right.shape, jnp.bfloat16),
            pltpu.VMEM(left.shape, jnp.bfloat16),
            pltpu.VMEM((BS, BS), jnp.float32),
            pltpu.VMEM((BS, BS), jnp.float32),
        ],
        compiler_params=pltpu.CompilerParams(vmem_limit_bytes=24 * 2**20),
        name="products",
    )(bank, tables, right, left)


def solution(mesh):
    return jax.shard_map(
        shards,
        mesh=mesh,
        in_specs=(
            P("blk", None, "pair", None),
            P(),
            P(),
            P(),
            P("blk", "pair", None, None),
            P("blk", "pair"),
        ),
        out_specs=P("blk", None, "pair", None),
        check_vma=False,
    )
```

```python
import jax
import jax.numpy as jnp
from jax import lax
from jax.experimental import pallas as pl
from jax.experimental.pallas import tpu as pltpu
from jax.sharding import PartitionSpec as P

BS = 128
NAUX = 4
OWN = 3
BAND = 3
NEAR = OWN + 2
FAR = OWN + 4
ROWS = 8
SCALE = 0.0078125
OWN_ROWS = (OWN * BAND + 1) * ROWS

LEFT_PAIRS = [(k, i) for k in range(NEAR) for i in range(OWN) if abs(i - (k - 1)) <= 1]
FIRST_LEFT = {pair: at for at, pair in enumerate(LEFT_PAIRS)}


def owners_of(near):
    return [i for i in range(OWN) if abs(i - (near - 1)) <= 1]


def holds_above(q):
    return ((lax.axis_index("blk") + q) & 1) == 0


def early():
    return lax.axis_index("pair") < 4


def make_factors(table_ref, right_ref, left_ref, rows_ref, cols_ref):
    own_first = lax.axis_index("blk") * OWN
    my_row = pl.multiple_of(lax.axis_index("pair") * ROWS, ROWS)
    nblk = (table_ref.shape[0] - OWN_ROWS) // (2 + NAUX)

    rows_ref[...] = jnp.zeros_like(rows_ref)
    for t in range(FAR):
        block = jnp.clip(own_first - 2 + t, 0, nblk - 1)
        rows_ref[t : t + 1, :] = table_ref[pl.ds(block, 1), :]
        offset = table_ref[pl.ds(nblk + block, 1), :]
        rows_ref[8 + t : 9 + t, :] = 2.0 * block.astype(jnp.float32) + offset
        for p in range(NAUX):
            weight = table_ref[pl.ds(2 * nblk + NAUX * block + p, 1), :]
            rows_ref[16 + 8 * p + t : 17 + 8 * p + t, :] = weight
    cols_ref[...] = rows_ref[...].T

    def tiles(columns, t_row, t_col):
        def column(quantity):
            at = 8 * quantity + t_row
            return columns[:, at : at + 1]

        def row(quantity):
            at = 8 * quantity + t_col
            return rows_ref[at : at + 1, :]

        e_r, e_c = column(0), row(0)
        reduced = e_r * e_c / (e_r + e_c)
        distance = column(1) - row(1)
        overlap = jnp.exp(-reduced * distance * distance)
        return [
            (overlap * jnp.tanh(column(2 + p) * row(2 + p))).astype(jnp.bfloat16)
            for p in range(NAUX)
        ]

    step = 32
    for t_far in range(FAR):
        for start in range(0, BS, step):
            columns = cols_ref[start : start + step, :]
            for near in range(NEAR):
                side = t_far - near
                if 0 <= side <= 2:
                    for p, tile in enumerate(tiles(columns, t_far, near + 1)):
                        at = (side * NAUX + p) * BS + start
                        right_ref[near, at : at + step, :] = tile

    mine = cols_ref[pl.ds(my_row, ROWS), :]
    for at, (near, own) in enumerate(LEFT_PAIRS):
        made = tiles(mine, own + 2, near + 1)
        left_ref[at * 32 : at * 32 + 32, :] = jnp.concatenate(made, axis=0)


def factors_kernel(table_ref, right_ref, left_ref, rows_ref, cols_ref):
    @pl.when(early())
    def _():
        make_factors(table_ref, right_ref, left_ref, rows_ref, cols_ref)


def products_kernel(
    bank_ref, table_ref, right_in, left_in, out_ref,
    half_ref, times_ref, mixed_ref, right_ref, left_ref, rows_ref, cols_ref
):
    @pl.when(early())
    def _():
        make_products(bank_ref, right_in, left_in, out_ref, half_ref, times_ref, mixed_ref)

    @pl.when(jnp.logical_not(early()))
    def _():
        make_factors(table_ref, right_ref, left_ref, rows_ref, cols_ref)
        make_products(bank_ref, right_ref, left_ref, out_ref, half_ref, times_ref, mixed_ref)


def make_products(bank_ref, right_ref, left_ref, out_ref, half_ref, times_ref, mixed_ref):
    devices = bank_ref.shape[0]

    def bank(near, c):
        if 0 < near < NEAR - 1:
            pieces = [bank_ref[q, (near - 1) * BAND + c] for q in range(devices)]
        else:
            holder = jnp.where(holds_above(0), 1, 0) if near == 0 else jnp.where(holds_above(0), 0, 1)
            pieces = [bank_ref[q // 2 * 2 + holder, OWN * BAND + 1 + 2 * c + q % 2] for q in range(devices)]
        return jnp.concatenate([piece.astype(jnp.float32) for piece in pieces], axis=0)

    own_first = lax.axis_index("blk") * OWN
    slot = lax.broadcasted_iota(jnp.int32, (1, BS), 1)
    code_row = lax.broadcasted_iota(jnp.int32, (BS, BS), 0)
    lists = bank_ref[:, OWN * BAND].astype(jnp.float32).astype(jnp.int32)
    found = jnp.zeros((BS, BS), jnp.float32)
    for q in range(lists.shape[0]):
        row_b, col_b, mid_b, far_b = (lists[q, n : n + 1, :] for n in range(4))
        length = lists[q, 4:5, 0:1]
        code = (
            (row_b - own_first) * 27 + (col_b - row_b + 1) * 9 + (mid_b - row_b + 1) * 3 + far_b - mid_b + 1
        )
        code = jnp.where(slot < length, code, BS)
        found += (code == code_row).astype(jnp.float32)
    times_ref[...] = jnp.dot(
        found.astype(jnp.bfloat16), jnp.ones((BS, BS), jnp.bfloat16), preferred_element_type=jnp.float32
    )

    for near in range(NEAR):
        density = jnp.concatenate([bank(near, c) for c in range(BAND)], axis=1)
        density = density.astype(jnp.bfloat16)
        owners = owners_of(near)
        at = FIRST_LEFT[(near, owners[0])] * 32
        size = len(owners) * 32
        half = jnp.dot(left_ref[at : at + size, :], density, preferred_element_type=jnp.float32)
        half_ref[at : at + size, :] = half.astype(jnp.bfloat16).astype(jnp.float32)

    for j in range(NEAR):
        owners = owners_of(j)
        for slot, i in enumerate(owners):
            for side in range(3):
                far = j - 1 + side
                total = [None] * NAUX
                for k in range(i, i + 3):
                    if abs(far - k) > 1:
                        continue
                    code = i * 27 + (j - i) * 9 + (k - i) * 3 + far - k + 1
                    times = times_ref[code : code + 1, :]
                    at = FIRST_LEFT[(k, i)] * 32
                    column = (far - k + 1) * BS
                    for p in range(NAUX):
                        piece = times * half_ref[
                            at + p * ROWS : at + (p + 1) * ROWS, column : column + BS
                        ]
                        total[p] = piece if total[p] is None else total[p] + piece
                for p in range(NAUX):
                    high = total[p].astype(jnp.bfloat16)
                    low = total[p] - high.astype(jnp.float32)
                    both = jnp.concatenate([high.astype(jnp.float32), low], axis=0)
                    column = (side * NAUX + p) * BS
                    mixed_ref[slot * 16 : slot * 16 + 16, column : column + BS] = both.astype(
                        jnp.bfloat16
                    )
        size = len(owners) * 16
        term = jnp.dot(mixed_ref[:size, :], right_ref[j], preferred_element_type=jnp.float32)
        for slot, i in enumerate(owners):
            pair = term[slot * 16 : slot * 16 + 8] + term[slot * 16 + 8 : slot * 16 + 16]
            out_ref[i, j - i] = pair * SCALE


def vmem(count):
    return [pl.BlockSpec(memory_space=pltpu.VMEM)] * count


def shards(density, exponents, offsets, expansion, quartet_list, list_length):
    count = lax.axis_size("blk")
    pairs = lax.axis_size("pair")
    second = (lax.axis_index("pair") & 1) == 1
    up = holds_above(lax.axis_index("pair"))

    other = lax.ppermute(density, "pair", [(q, q ^ 1) for q in range(pairs)])

    nblk = exponents.shape[0] // BS
    pieces = [
        exponents.reshape(nblk, BS),
        offsets.reshape(nblk, BS),
        expansion.reshape(NAUX, nblk, BS).transpose(1, 0, 2).reshape(NAUX * nblk, BS),
        density.reshape(OWN * BAND * ROWS, BS),
        quartet_list[0, 0],
        list_length,
    ]
    rows, tables, at = (2 + NAUX) * nblk + OWN_ROWS, 0.0, 0
    for piece in pieces:
        high, wide = piece.shape
        tables += jnp.pad(piece, ((at, rows - at - high), (0, BS - wide))).astype(jnp.float32)
        at += high
    tables = lax.optimization_barrier(tables)
    own = tables[-OWN_ROWS:].astype(jnp.bfloat16).reshape(OWN * BAND + 1, ROWS, BS)
    mine = jnp.where(up, own[(OWN - 1) * BAND : OWN * BAND], own[:BAND])
    theirs = jnp.where(up, other[OWN - 1], other[0])
    facing = jnp.where(second, jnp.stack([theirs, mine], axis=1), jnp.stack([mine, theirs], axis=1))
    ups = [
        (b * pairs + q, (b + 1) * pairs + q) for b in range(count - 1) for q in range(pairs) if (b + q) % 2 == 0
    ]
    halo = lax.ppermute(facing, ("blk", "pair"), ups + [(high, low) for low, high in ups])

    right, left = pl.pallas_call(
        factors_kernel,
        out_shape=(
            jax.ShapeDtypeStruct((NEAR, 3 * NAUX * BS, BS), jnp.bfloat16),
            jax.ShapeDtypeStruct((len(LEFT_PAIRS) * NAUX * ROWS, BS), jnp.bfloat16),
        ),
        in_specs=vmem(1),
        out_specs=tuple(vmem(2)),
        scratch_shapes=[pltpu.VMEM((BS, BS), jnp.float32), pltpu.VMEM((BS, BS), jnp.float32)],
        compiler_params=pltpu.CompilerParams(vmem_limit_bytes=24 * 2**20),
        cost_estimate=pl.CostEstimate(flops=30_000_000, bytes_accessed=3_000_000, transcendentals=1_500_000),
        name="factors",
    )(tables)

    payload = jnp.concatenate([own, halo.reshape(BAND * 2, ROWS, BS)], axis=0)
    payload, right, left = lax.optimization_barrier((payload, right, left))
    bank = lax.all_gather(payload, "pair", axis=0)

    return pl.pallas_call(
        products_kernel,
        out_shape=jax.ShapeDtypeStruct((OWN, BAND, ROWS, BS), jnp.float32),
        in_specs=vmem(4),
        out_specs=pl.BlockSpec(memory_space=pltpu.VMEM),
        scratch_shapes=[
            pltpu.VMEM((len(LEFT_PAIRS) * NAUX * ROWS, BAND * BS), jnp.float32),
            pltpu.VMEM((BS, BS), jnp.float32),
            pltpu.VMEM((3 * 16, 3 * NAUX * BS), jnp.bfloat16),
            pltpu.VMEM(right.shape, jnp.bfloat16),
            pltpu.VMEM(left.shape, jnp.bfloat16),
            pltpu.VMEM((BS, BS), jnp.float32),
            pltpu.VMEM((BS, BS), jnp.float32),
        ],
        compiler_params=pltpu.CompilerParams(vmem_limit_bytes=24 * 2**20),
        name="products",
    )(bank, tables, right, left)


def solution(mesh):
    return jax.shard_map(
        shards,
        mesh=mesh,
        in_specs=(
            P("blk", None, "pair", None),
            P(),
            P(),
            P(),
            P("blk", "pair", None, None),
            P("blk", "pair"),
        ),
        out_specs=P("blk", None, "pair", None),
        check_vma=False,
    )
```

```python
import jax
import jax.numpy as jnp
from jax import lax
from jax.experimental import pallas as pl
from jax.experimental.pallas import tpu as pltpu
from jax.sharding import PartitionSpec as P

BS = 128
NAUX = 4
OWN = 3
BAND = 3
NEAR = OWN + 2
FAR = OWN + 4
ROWS = 8
SCALE = 0.0078125
OWN_ROWS = (OWN * BAND + 1) * ROWS

LEFT_PAIRS = [(k, i) for k in range(NEAR) for i in range(OWN) if abs(i - (k - 1)) <= 1]
FIRST_LEFT = {pair: at for at, pair in enumerate(LEFT_PAIRS)}


def owners_of(near):
    return [i for i in range(OWN) if abs(i - (near - 1)) <= 1]


def holds_above(q):
    return ((lax.axis_index("blk") + q) & 1) == 0


def early():
    return lax.axis_index("pair") < 4


def make_factors(table_ref, right_ref, left_ref, rows_ref, cols_ref):
    own_first = lax.axis_index("blk") * OWN
    my_row = pl.multiple_of(lax.axis_index("pair") * ROWS, ROWS)
    nblk = (table_ref.shape[0] - OWN_ROWS) // (2 + NAUX)

    rows_ref[...] = jnp.zeros_like(rows_ref)
    for t in range(FAR):
        block = jnp.clip(own_first - 2 + t, 0, nblk - 1)
        rows_ref[t : t + 1, :] = table_ref[pl.ds(block, 1), :]
        offset = table_ref[pl.ds(nblk + block, 1), :]
        rows_ref[8 + t : 9 + t, :] = 2.0 * block.astype(jnp.float32) + offset
        for p in range(NAUX):
            weight = table_ref[pl.ds(2 * nblk + NAUX * block + p, 1), :]
            rows_ref[16 + 8 * p + t : 17 + 8 * p + t, :] = weight
    cols_ref[...] = rows_ref[...].T

    def tiles(columns, t_row, t_col):
        def column(quantity):
            at = 8 * quantity + t_row
            return columns[:, at : at + 1]

        def row(quantity):
            at = 8 * quantity + t_col
            return rows_ref[at : at + 1, :]

        e_r, e_c = column(0), row(0)
        reduced = e_r * e_c / (e_r + e_c)
        distance = column(1) - row(1)
        overlap = jnp.exp(-reduced * distance * distance)
        return [
            (overlap * jnp.tanh(column(2 + p) * row(2 + p))).astype(jnp.bfloat16)
            for p in range(NAUX)
        ]

    step = 32
    for t_far in range(FAR):
        for start in range(0, BS, step):
            columns = cols_ref[start : start + step, :]
            for near in range(NEAR):
                side = t_far - near
                if 0 <= side <= 2:
                    for p, tile in enumerate(tiles(columns, t_far, near + 1)):
                        at = (side * NAUX + p) * BS + start
                        right_ref[near, at : at + step, :] = tile

    mine = cols_ref[pl.ds(my_row, ROWS), :]
    for at, (near, own) in enumerate(LEFT_PAIRS):
        made = tiles(mine, own + 2, near + 1)
        left_ref[at * 32 : at * 32 + 32, :] = jnp.concatenate(made, axis=0)


def factors_kernel(table_ref, right_ref, left_ref, rows_ref, cols_ref):
    @pl.when(early())
    def _():
        make_factors(table_ref, right_ref, left_ref, rows_ref, cols_ref)


def products_kernel(
    bank_ref, table_ref, right_in, left_in, out_ref,
    half_ref, times_ref, mixed_ref, right_ref, left_ref, rows_ref, cols_ref
):
    @pl.when(early())
    def _():
        make_products(bank_ref, right_in, left_in, out_ref, half_ref, times_ref, mixed_ref)

    @pl.when(jnp.logical_not(early()))
    def _():
        make_factors(table_ref, right_ref, left_ref, rows_ref, cols_ref)
        make_products(bank_ref, right_ref, left_ref, out_ref, half_ref, times_ref, mixed_ref)


def make_products(bank_ref, right_ref, left_ref, out_ref, half_ref, times_ref, mixed_ref):
    devices = bank_ref.shape[0]

    def bank(near, c):
        if 0 < near < NEAR - 1:
            pieces = [bank_ref[q, (near - 1) * BAND + c] for q in range(devices)]
        else:
            holder = jnp.where(holds_above(0), 1, 0) if near == 0 else jnp.where(holds_above(0), 0, 1)
            pieces = [bank_ref[q // 2 * 2 + holder, OWN * BAND + 1 + 2 * c + q % 2] for q in range(devices)]
        return jnp.concatenate([piece.astype(jnp.float32) for piece in pieces], axis=0)

    own_first = lax.axis_index("blk") * OWN
    slot = lax.broadcasted_iota(jnp.int32, (1, BS), 1)
    code_row = lax.broadcasted_iota(jnp.int32, (BS, BS), 0)
    lists = bank_ref[:, OWN * BAND].astype(jnp.float32).astype(jnp.int32)
    found = jnp.zeros((BS, BS), jnp.float32)
    for q in range(lists.shape[0]):
        row_b, col_b, mid_b, far_b = (lists[q, n : n + 1, :] for n in range(4))
        length = lists[q, 4:5, 0:1]
        code = (
            (row_b - own_first) * 27 + (col_b - row_b + 1) * 9 + (mid_b - row_b + 1) * 3 + far_b - mid_b + 1
        )
        code = jnp.where(slot < length, code, BS)
        found += (code == code_row).astype(jnp.float32)
    times_ref[...] = jnp.dot(
        found.astype(jnp.bfloat16), jnp.ones((BS, BS), jnp.bfloat16), preferred_element_type=jnp.float32
    )

    for near in range(NEAR):
        density = jnp.concatenate([bank(near, c) for c in range(BAND)], axis=1)
        density = density.astype(jnp.bfloat16)
        owners = owners_of(near)
        at = FIRST_LEFT[(near, owners[0])] * 32
        size = len(owners) * 32
        half = jnp.dot(left_ref[at : at + size, :], density, preferred_element_type=jnp.float32)
        half_ref[at : at + size, :] = half.astype(jnp.bfloat16).astype(jnp.float32)

    for j in range(NEAR):
        owners = owners_of(j)
        for slot, i in enumerate(owners):
            for side in range(3):
                far = j - 1 + side
                total = [None] * NAUX
                for k in range(i, i + 3):
                    if abs(far - k) > 1:
                        continue
                    code = i * 27 + (j - i) * 9 + (k - i) * 3 + far - k + 1
                    times = times_ref[code : code + 1, :]
                    at = FIRST_LEFT[(k, i)] * 32
                    column = (far - k + 1) * BS
                    for p in range(NAUX):
                        piece = times * half_ref[
                            at + p * ROWS : at + (p + 1) * ROWS, column : column + BS
                        ]
                        total[p] = piece if total[p] is None else total[p] + piece
                for p in range(NAUX):
                    high = total[p].astype(jnp.bfloat16)
                    low = total[p] - high.astype(jnp.float32)
                    both = jnp.concatenate([high.astype(jnp.float32), low], axis=0)
                    column = (side * NAUX + p) * BS
                    mixed_ref[slot * 16 : slot * 16 + 16, column : column + BS] = both.astype(
                        jnp.bfloat16
                    )
        size = len(owners) * 16
        term = jnp.dot(mixed_ref[:size, :], right_ref[j], preferred_element_type=jnp.float32)
        for slot, i in enumerate(owners):
            pair = term[slot * 16 : slot * 16 + 8] + term[slot * 16 + 8 : slot * 16 + 16]
            out_ref[i, j - i] = pair * SCALE


def vmem(count):
    return [pl.BlockSpec(memory_space=pltpu.VMEM)] * count


def shards(density, exponents, offsets, expansion, quartet_list, list_length):
    count = lax.axis_size("blk")
    pairs = lax.axis_size("pair")
    second = (lax.axis_index("pair") & 1) == 1
    up = holds_above(lax.axis_index("pair"))

    other = lax.ppermute(density, "pair", [(q, q ^ 1) for q in range(pairs)])

    mine = jnp.where(up, density[OWN - 1], density[0])
    theirs = jnp.where(up, other[OWN - 1], other[0])
    facing = jnp.where(second, jnp.stack([theirs, mine], axis=1), jnp.stack([mine, theirs], axis=1))
    facing, exponents, offsets, expansion, quartet_list = lax.optimization_barrier(
        (facing, exponents, offsets, expansion, quartet_list)
    )

    nblk = exponents.shape[0] // BS
    pieces = [
        exponents.reshape(nblk, BS),
        offsets.reshape(nblk, BS),
        expansion.reshape(NAUX, nblk, BS).transpose(1, 0, 2).reshape(NAUX * nblk, BS),
        density.reshape(OWN * BAND * ROWS, BS),
        quartet_list[0, 0],
        list_length,
    ]
    rows, tables, at = (2 + NAUX) * nblk + OWN_ROWS, 0.0, 0
    for piece in pieces:
        high, wide = piece.shape
        tables += jnp.pad(piece, ((at, rows - at - high), (0, BS - wide))).astype(jnp.float32)
        at += high
    tables = lax.optimization_barrier(tables)
    own = tables[-OWN_ROWS:].astype(jnp.bfloat16).reshape(OWN * BAND + 1, ROWS, BS)
    ups = [
        (b * pairs + q, (b + 1) * pairs + q) for b in range(count - 1) for q in range(pairs) if (b + q) % 2 == 0
    ]
    halo = lax.ppermute(facing, ("blk", "pair"), ups + [(high, low) for low, high in ups])

    right, left = pl.pallas_call(
        factors_kernel,
        out_shape=(
            jax.ShapeDtypeStruct((NEAR, 3 * NAUX * BS, BS), jnp.bfloat16),
            jax.ShapeDtypeStruct((len(LEFT_PAIRS) * NAUX * ROWS, BS), jnp.bfloat16),
        ),
        in_specs=vmem(1),
        out_specs=tuple(vmem(2)),
        scratch_shapes=[pltpu.VMEM((BS, BS), jnp.float32), pltpu.VMEM((BS, BS), jnp.float32)],
        compiler_params=pltpu.CompilerParams(vmem_limit_bytes=24 * 2**20),
        cost_estimate=pl.CostEstimate(flops=30_000_000, bytes_accessed=3_000_000, transcendentals=1_500_000),
        name="factors",
    )(tables)

    payload = jnp.concatenate([own, halo.reshape(BAND * 2, ROWS, BS)], axis=0)
    payload, right, left = lax.optimization_barrier((payload, right, left))
    bank = lax.all_gather(payload, "pair", axis=0)

    return pl.pallas_call(
        products_kernel,
        out_shape=jax.ShapeDtypeStruct((OWN, BAND, ROWS, BS), jnp.float32),
        in_specs=vmem(4),
        out_specs=pl.BlockSpec(memory_space=pltpu.VMEM),
        scratch_shapes=[
            pltpu.VMEM((len(LEFT_PAIRS) * NAUX * ROWS, BAND * BS), jnp.float32),
            pltpu.VMEM((BS, BS), jnp.float32),
            pltpu.VMEM((3 * 16, 3 * NAUX * BS), jnp.bfloat16),
            pltpu.VMEM(right.shape, jnp.bfloat16),
            pltpu.VMEM(left.shape, jnp.bfloat16),
            pltpu.VMEM((BS, BS), jnp.float32),
            pltpu.VMEM((BS, BS), jnp.float32),
        ],
        compiler_params=pltpu.CompilerParams(vmem_limit_bytes=24 * 2**20),
        name="products",
    )(bank, tables, right, left)


def solution(mesh):
    return jax.shard_map(
        shards,
        mesh=mesh,
        in_specs=(
            P("blk", None, "pair", None),
            P(),
            P(),
            P(),
            P("blk", "pair", None, None),
            P("blk", "pair"),
        ),
        out_specs=P("blk", None, "pair", None),
        check_vma=False,
    )
```
